32 devices in a mesh: slab: 8 (over z, y), rep: 4 (over x, core).
Axes of the slice: x: 2, y: 2, z: 4, core: 2. Of those that a mesh axis runs over, the one named last changes fastest.
Arguments:
- saved_input: bfloat16 [4, 6, 1, 256, 256, 256], P('rep', None, None, 'slab'), may hold values from -6 to 6
- output_grad: bfloat16 [4, 6, 1, 256, 256, 256], P('rep', None, None, 'slab'), may hold values from -6 to 6
- spectral_weight: float32 [1024, 8, 1, 1, 32], P('slab'), may hold values from -18 to 18
- bypass_weight: float32 [8, 1, 1], replicated, may hold values from -1.8 to 1.8
Outputs:
- input_grad: bfloat16 [4, 6, 1, 256, 256, 256], P('rep', None, None, 'slab')
- weight_grad: float32 [1024, 8, 1, 1, 32], P('slab')
The draws below stay inside these ranges and needn't reach their ends.
All inputs are finite; a program needn't handle non-finite values.
Results may differ from the reference program's by a relative error of at most 0.001.
Values sent between devices are 32-bit elements; how exact they have to be, the bound alone decides.
A program may use at most 320 MiB of HBM per device.

```python
import jax
import jax.numpy as jnp

NX = 256
NY = 256
NZ = 256
KM = 32
CH = 1
SAMPLES = 4


def block_scale(rng, dims, split, low, top_value):
    level, own = 1.0, jax.random.fold_in(rng, 6)
    for dim, parts in split:
        heights = jnp.exp(jax.random.uniform(jax.random.fold_in(own, dim), (parts,), jnp.float32, low / len(split), top_value / len(split)))
        level = level * jnp.repeat(heights, dims[dim] // parts).reshape([-1 if axis == dim else 1 for axis in range(len(dims))])
    return level


def centred(rng, extent, width, most, cuts=(), kind=jnp.bfloat16):
    drawn = jax.random.normal(rng, extent, jnp.float32) * width
    if len(cuts) > 0:
        drawn = block_scale(rng, extent, cuts, -0.22, 0.18) * drawn
    return jnp.clip(drawn, min=-most, max=most).astype(kind)


def setup_inputs(seed: int = 0) -> dict:
    streams_of = jax.random.split(jax.random.key(seed), 5)
    return {
        "saved_input": centred(streams_of[0], (SAMPLES, 6, CH, NZ, NX, NY), 1.0, 6.0, ((0, 4), (3, 8))),
        "output_grad": centred(streams_of[1], (SAMPLES, 6, CH, NZ, NX, NY), 1.0, 6.0, ((0, 4), (3, 8))),
        "spectral_weight": centred(streams_of[2], (KM * KM, 8, CH, CH, KM), 3.0, 18.0, ((0, 8),), jnp.float32),
        "bypass_weight": centred(streams_of[3], (8, CH, CH), 0.3, 1.8, (), jnp.float32),
    }


def kept(length):
    counter = jnp.arange(KM)
    return jnp.where(counter < KM // 2, counter, length - KM + counter)


def to_complex(field):
    widened = field.astype(jnp.float32)
    return widened[:3] + 1j * widened[3:]


def forward_modes(field):
    spectrum = jnp.fft.fftn(to_complex(field), axes=(2, 3, 4), norm="ortho")
    spectrum = spectrum[:, :, kept(NZ)][:, :, :, kept(NX)][:, :, :, :, kept(NY)]
    return jnp.transpose(spectrum, (3, 4, 0, 1, 2)).reshape(KM * KM, 3, CH, KM)


def reference(saved_input, output_grad, spectral_weight, bypass_weight):
    w_scalar = spectral_weight[:, 0] + 1j * spectral_weight[:, 4]
    w_vector = spectral_weight[:, 1:4] + 1j * spectral_weight[:, 5:8]
    b_scalar = bypass_weight[0] + 1j * bypass_weight[4]
    b_vector = bypass_weight[1:4] + 1j * bypass_weight[5:8]
    depth_index = kept(NZ)[:, None, None]
    first_index = kept(NX)[None, :, None]
    second_index = kept(NY)[None, None, :]
    scalar_grad = jnp.zeros((KM * KM, CH, CH, KM), jnp.float32)
    vector_grad = jnp.zeros((KM * KM, 3, CH, CH, KM), jnp.float32)
    outputs = []
    for sample in range(SAMPLES):
        inputs = forward_modes(saved_input[sample])
        grads = forward_modes(output_grad[sample])
        scalar_grad = scalar_grad + jnp.einsum("rkim,rkom->roim", jnp.conj(inputs), grads)
        vector_grad = vector_grad - 1j * jnp.cross(jnp.conj(inputs)[:, :, None, :, :], grads[:, :, :, None, :], axis=1)
        mode_grads = jnp.einsum("roim,rkom->rkim", jnp.conj(w_scalar), grads)
        mode_grads = mode_grads + 1j * jnp.sum(jnp.cross(jnp.conj(w_vector), grads[:, :, :, None, :], axis=1), axis=2)
        cube = jnp.transpose(mode_grads.reshape(KM, KM, 3, CH, KM), (2, 3, 4, 0, 1))
        full = jnp.zeros((3, CH, NZ, NX, NY), cube.dtype)
        full = full.at[:, :, depth_index, first_index, second_index].set(cube)
        spectral = jnp.fft.ifftn(full, axes=(2, 3, 4), norm="ortho")
        cotangent = to_complex(output_grad[sample])
        bypass = jnp.einsum("oi,kozxy->kizxy", jnp.conj(b_scalar), cotangent)
        columns = []
        for target in range(CH):
            term = 0.0
            for source in range(CH):
                term = term + 1j * jnp.cross(jnp.conj(b_vector[:, source, target])[:, None, None, None], cotangent[:, source], axis=0)
            columns.append(term)
        bypass = bypass + jnp.stack(columns, axis=1)
        summed = spectral + bypass
        outputs.append(jnp.concatenate([jnp.real(summed), jnp.imag(summed)], axis=0).astype(jnp.bfloat16))
    input_grad = jnp.stack(outputs)
    weight_grad = jnp.concatenate([jnp.real(scalar_grad)[:, None], jnp.real(vector_grad), jnp.imag(scalar_grad)[:, None], jnp.imag(vector_grad)], axis=1)
    return input_grad, weight_grad.astype(jnp.float32)
```

```python
import functools
import math

import jax
import jax.numpy as jnp
import numpy as np
from jax import lax
from jax.experimental import pallas as pl
from jax.experimental.pallas import tpu as pltpu
from jax.sharding import PartitionSpec as P

NZ = 256
KM = 32
F32 = jnp.float32
BF16 = jnp.bfloat16


def table(length):
    counter = np.arange(KM)
    freqs = np.where(counter < KM // 2, counter, counter - KM)
    angles = (np.arange(length)[:, None] * freqs[None, :] % length) * (2.0 * math.pi / length)
    return np.cos(angles), np.sin(angles)


def halves(values):
    values = np.asarray(values, np.float32)
    high = values.astype(BF16)
    return high, (values - high.astype(np.float32)).astype(BF16)


def split(values):
    high = values.astype(BF16)
    return high, (values - high.astype(F32)).astype(BF16)


def dot(left, right):
    return jnp.dot(left, right, preferred_element_type=F32)


def turn(values, sign):
    half = values.shape[-1] // 2
    return jnp.concatenate([-sign * values[..., half:], sign * values[..., :half]], axis=-1)


class Plan:
    def __init__(self, nx, ny, planes, rows_owned):
        self.nx, self.ny, self.planes = nx, ny, planes
        self.zb = min(8, planes)
        self.shares = max(1, KM // rows_owned)
        per_owner = max(1, rows_owned // KM)
        self.lane_groups = min(2, per_owner)
        self.owned_pairs = per_owner // self.lane_groups
        self.owners = KM // per_owner
        self.pairs = KM // self.lane_groups
        self.lanes = 2 * self.lane_groups * KM
        groups = self.lane_groups
        factor = 1.0 / math.sqrt(nx * ny * NZ)
        cos_x, sin_x = table(nx)
        cos_y, sin_y = table(ny)
        order = np.concatenate([np.arange(g, KM, groups) for g in range(groups)])
        cos_x, sin_x = cos_x[:, order], sin_x[:, order]
        from_real = np.concatenate([cos_x.T, -sin_x.T], 0) * factor
        from_imag = np.concatenate([sin_x.T, cos_x.T], 0) * factor
        self.fwd_x = np.stack(
            [np.concatenate(halves(from_real), 0), np.concatenate(halves(from_imag), 0)], 0
        )
        fwd_y = np.zeros((2, groups, ny, 2, groups, KM))
        inv_y = np.zeros((2, groups, KM, 2, groups, ny))
        for g in range(groups):
            fwd_y[0, g, :, 0, g] = cos_y
            fwd_y[0, g, :, 1, g] = -sin_y
            fwd_y[1, g, :, 0, g] = sin_y
            fwd_y[1, g, :, 1, g] = cos_y
            inv_y[0, g, :, 0, g] = cos_y.T
            inv_y[0, g, :, 1, g] = sin_y.T
            inv_y[1, g, :, 0, g] = -sin_y.T
            inv_y[1, g, :, 1, g] = cos_y.T
        fwd_y = fwd_y.reshape(2 * groups, ny, self.lanes)
        self.fwd_y = np.concatenate(halves(fwd_y), -1)
        inv_y = inv_y.reshape(self.lanes, 2 * groups * ny)
        inv_high, inv_low = halves(inv_y)
        self.inv_y = np.concatenate([inv_high, inv_high, inv_low], 0)
        inv_x = np.concatenate(
            [np.concatenate([cos_x, -sin_x], 1), np.concatenate([sin_x, cos_x], 1)], 0
        ) * factor
        high, low = halves(inv_x)
        self.inv_x = np.concatenate([high, high, low], 1)
        cos_z, sin_z = table(NZ)
        self.fwd_z = np.stack(halves(np.concatenate([cos_z, sin_z], 1)), 0)


def forward_kernel(plan, field, tab_x, tab_y, tab_z, out, along_x, along_xy):
    group = pl.program_id(1)
    rows = 2 * KM
    pairs, lanes, zb = plan.pairs, plan.lanes, plan.zb
    for z in range(zb):
        both = dot(tab_x[0], field[0, 0, z]) + dot(tab_x[1], field[1, 0, z])
        summed = both[:rows] + both[rows:]
        for part in range(plan.ny // 128):
            along_x[part, pl.ds(z, rows, stride=zb), :] = summed[:, part * 128 : part * 128 + 128]
    block = pairs * zb
    wide, narrow = 0.0, 0.0
    for g in range(rows // pairs):
        values = jnp.concatenate(
            [along_x[part, g * block : (g + 1) * block] for part in range(plan.ny // 128)], axis=1
        )
        high, low = split(values)
        wide = wide + dot(high, tab_y[g])
        narrow = narrow + dot(low, tab_y[g, :, :lanes])
    modes = wide[:, :lanes] + wide[:, lanes:] + narrow
    along_xy[:, pl.ds(pl.multiple_of(group * zb, zb), zb), :] = modes.reshape(pairs, zb, lanes)

    @pl.when(group == plan.planes // plan.zb - 1)
    def _():
        for pair in range(pairs):
            high, low = split(along_xy[pair])
            turned = dot(tab_z[0], high) + dot(tab_z[1], high) + dot(tab_z[0], low)
            out[pair // plan.owned_pairs, 0, pair % plan.owned_pairs] = turned[:KM] + turn(
                turned[KM:], -1.0
            )


def forward_modes(plan, field, tab_z):
    planes, nx, ny = plan.planes, plan.nx, plan.ny
    whole = lambda k, g: (0, 0, 0)
    return pl.pallas_call(
        functools.partial(forward_kernel, plan),
        grid=(3, planes // plan.zb),
        in_specs=[
            pl.BlockSpec((2, 1, plan.zb, nx, ny), lambda k, g: (0, k, g, 0, 0)),
            pl.BlockSpec(plan.fwd_x.shape, whole),
            pl.BlockSpec(plan.fwd_y.shape, whole),
            pl.BlockSpec((2, 2 * KM, planes), whole),
        ],
        out_specs=pl.BlockSpec(
            (plan.owners, 1, plan.owned_pairs, KM, plan.lanes), lambda k, g: (0, k, 0, 0, 0)
        ),
        out_shape=jax.ShapeDtypeStruct(
            (plan.owners, 3, plan.owned_pairs, KM, plan.lanes), F32
        ),
        scratch_shapes=[
            pltpu.VMEM((ny // 128, 2 * KM * plan.zb, 128), F32),
            pltpu.VMEM((plan.pairs, planes, plan.lanes), F32),
        ],
        compiler_params=pltpu.CompilerParams(vmem_limit_bytes=40 * 2**20),
        cost_estimate=pl.CostEstimate(
            flops=2 * 6 * planes * nx * ny * 128, bytes_accessed=12 * planes * nx * ny,
            transcendentals=0,
        ),
    )(field, jnp.asarray(plan.fwd_x), jnp.asarray(plan.fwd_y), tab_z)


def bypass_terms(weight, real, imag):
    s_r, s_i = weight[0], weight[4]
    v_r = [weight[1 + axis] for axis in range(3)]
    v_i = [weight[5 + axis] for axis in range(3)]
    outs_r, outs_i = [], []
    for k in range(3):
        a, b = (k + 1) % 3, (k + 2) % 3
        cross_r = (
            v_r[a] * real[b] - v_r[b] * real[a] + v_i[a] * imag[b] - v_i[b] * imag[a]
        )
        cross_i = (
            v_r[a] * imag[b] - v_r[b] * imag[a] - v_i[a] * real[b] + v_i[b] * real[a]
        )
        outs_r.append(s_r * real[k] + s_i * imag[k] - cross_i)
        outs_i.append(s_r * imag[k] - s_i * real[k] + cross_r)
    return outs_r, outs_i


def inverse_kernel(
    plan, step_planes, weight, field, modes, tab_z, tab_y, tab_x, out, along_z, along_zy, spectral
):
    step = pl.program_id(0)
    pairs, lanes, nx, ny, zb = plan.pairs, plan.lanes, plan.nx, plan.ny, plan.zb
    steps = zb // step_planes
    block = pairs * zb

    @pl.when(step == 0)
    def _():
        for pair in range(pairs):
            for k in range(3):
                values = modes[pair // plan.owned_pairs, k, pair % plan.owned_pairs]
                high, low = split(jnp.concatenate([values, turn(values, 1.0)], axis=0))
                along_z[k, pair] = dot(tab_z[0], high) + dot(tab_z[1], high) + dot(tab_z[0], low)

    @pl.when(step % steps == 0)
    def _():
        start = pl.multiple_of(step * step_planes, zb)
        for k in range(3):
            values = along_z[k, :, pl.ds(start, zb), :].reshape(block, lanes)
            high, low = split(values)
            parts = jnp.concatenate([high, low, high], axis=1)
            for g in range(2 * plan.lane_groups):
                result = dot(parts, tab_y[:, g * ny : (g + 1) * ny])
                for part in range(ny // 128):
                    along_zy[k, part, g * block : (g + 1) * block] = result[
                        :, part * 128 : part * 128 + 128
                    ]

    for z in range(step_planes):
        where = (step % steps) * step_planes + z
        for k in range(3):
            values = jnp.concatenate(
                [
                    along_zy[k, part, pl.ds(where, 2 * KM, stride=zb), :]
                    for part in range(ny // 128)
                ],
                axis=1,
            )
            high, low = split(values)
            spectral[z, k] = dot(tab_x[...], jnp.concatenate([high, low, high], axis=0))
        for row in range(0, nx, 16):
            for lane in range(0, ny, 128):
                rows, columns = pl.ds(row, 16), pl.ds(lane, 128)
                real = [field[k, z, rows, columns].astype(F32) for k in range(3)]
                imag = [field[3 + k, z, rows, columns].astype(F32) for k in range(3)]
                outs_r, outs_i = bypass_terms(weight, real, imag)
                for k in range(3):
                    out[k, z, rows, columns] = (outs_r[k] + spectral[z, k, rows, columns]).astype(
                        BF16
                    )
                    out[3 + k, z, rows, columns] = (
                        outs_i[k] + spectral[z, k, pl.ds(nx + row, 16), columns]
                    ).astype(BF16)


def inverse_field(plan, weight, field, modes, tab_z):
    planes, nx, ny = plan.planes, plan.nx, plan.ny
    step_planes = 2
    whole = lambda i: (0, 0)
    return pl.pallas_call(
        functools.partial(inverse_kernel, plan, step_planes),
        grid=(planes // step_planes,),
        in_specs=[
            pl.BlockSpec(memory_space=pltpu.SMEM),
            pl.BlockSpec((6, step_planes, nx, ny), lambda i: (0, i, 0, 0)),
            pl.BlockSpec(modes.shape, lambda i: (0, 0, 0, 0, 0)),
            pl.BlockSpec((2, planes, 2 * KM), lambda i: (0, 0, 0)),
            pl.BlockSpec(plan.inv_y.shape, whole),
            pl.BlockSpec(plan.inv_x.shape, whole),
        ],
        out_specs=pl.BlockSpec((6, step_planes, nx, ny), lambda i: (0, i, 0, 0)),
        out_shape=jax.ShapeDtypeStruct((6, planes, nx, ny), BF16),
        scratch_shapes=[
            pltpu.VMEM((3, plan.pairs, planes, plan.lanes), F32),
            pltpu.VMEM((3, ny // 128, 2 * KM * plan.zb, 128), F32),
            pltpu.VMEM((step_planes, 3, 2 * nx, ny), F32),
        ],
        compiler_params=pltpu.CompilerParams(vmem_limit_bytes=40 * 2**20),
        cost_estimate=pl.CostEstimate(
            flops=2 * 6 * planes * nx * ny * 192, bytes_accessed=24 * planes * nx * ny,
            transcendentals=0,
        ),
    )(weight, field, modes, tab_z, jnp.asarray(plan.inv_y), jnp.asarray(plan.inv_x))


def shards(saved_input, output_grad, spectral_weight, bypass_weight):
    planes, nx, ny = saved_input.shape[3:]
    rows_owned = spectral_weight.shape[0]
    plan = Plan(nx, ny, planes, rows_owned)
    shares = plan.shares
    start = lax.axis_index("slab") * planes
    depth = lax.dynamic_slice_in_dim(jnp.asarray(plan.fwd_z), start, planes, axis=1)
    tab_fwd = jnp.swapaxes(depth, 1, 2)

    def spectrum(field):
        parts = forward_modes(plan, field.reshape(2, 3, planes, nx, ny), tab_fwd)
        if shares > 1:
            parts = parts.reshape(plan.owners, 3, 1, KM, 2, shares, KM // shares)
            parts = jnp.transpose(parts, (0, 5, 1, 2, 3, 4, 6))
            parts = parts.reshape(plan.owners * shares, 3, 1, KM, plan.lanes // shares)
        return lax.psum_scatter(parts, "slab", scatter_dimension=0, tiled=True)[0]

    grads = spectrum(output_grad)
    half = plan.lanes // (2 * shares)
    weights = spectral_weight.reshape(plan.owned_pairs, half, 8, KM)
    weights = jnp.transpose(weights, (2, 0, 3, 1))
    grads_r = [grads[k, :, :, :half] for k in range(3)]
    grads_i = [grads[k, :, :, half:] for k in range(3)]
    mode_r, mode_i = bypass_terms(weights, grads_r, grads_i)
    mode_grads = jnp.stack([jnp.concatenate([r, i], -1) for r, i in zip(mode_r, mode_i)], 0)
    modes = lax.all_gather(mode_grads, "slab", axis=0)
    if shares > 1:
        modes = modes.reshape(plan.owners, shares, 3, 1, KM, 2, KM // shares)
        modes = jnp.transpose(modes, (0, 2, 3, 4, 5, 1, 6))
        modes = modes.reshape(plan.owners, 3, 1, KM, plan.lanes)
    inputs = spectrum(saved_input)
    inputs_r = [inputs[k, :, :, :half] for k in range(3)]
    inputs_i = [inputs[k, :, :, half:] for k in range(3)]
    scalar_r = sum(inputs_r[k] * grads_r[k] + inputs_i[k] * grads_i[k] for k in range(3))
    scalar_i = sum(inputs_r[k] * grads_i[k] - inputs_i[k] * grads_r[k] for k in range(3))
    vector_r, vector_i = [], []
    for k in range(3):
        a, b = (k + 1) % 3, (k + 2) % 3
        vector_r.append(
            inputs_r[a] * grads_i[b] - inputs_r[b] * grads_i[a]
            - inputs_i[a] * grads_r[b] + inputs_i[b] * grads_r[a]
        )
        vector_i.append(
            inputs_r[b] * grads_r[a] - inputs_r[a] * grads_r[b]
            + inputs_i[b] * grads_i[a] - inputs_i[a] * grads_i[b]
        )
    local = jnp.stack([scalar_r] + vector_r + [scalar_i] + vector_i, axis=0)
    local = jnp.transpose(local, (1, 3, 0, 2)).reshape(rows_owned, 8, 1, 1, KM)
    weight_grad = lax.psum(local, "rep")
    input_grad = inverse_field(
        plan, bypass_weight.reshape(8), output_grad.reshape(6, planes, nx, ny), modes, depth
    )
    return (input_grad.reshape(1, 6, 1, planes, nx, ny), weight_grad)


def solution(mesh):
    placed = (
        P("rep", None, None, "slab", None, None),
        P("rep", None, None, "slab", None, None),
        P("slab", None, None, None, None),
        P(),
    )
    return jax.shard_map(
        shards,
        mesh=mesh,
        in_specs=placed,
        out_specs=(P("rep", None, None, "slab", None, None), P("slab", None, None, None, None)),
        check_vma=False,
    )
```

```python
import functools
import math

import jax
import jax.numpy as jnp
import numpy as np
from jax import lax
from jax.experimental import pallas as pl
from jax.experimental.pallas import tpu as pltpu
from jax.sharding import PartitionSpec as P

NZ = 256
KM = 32
F32 = jnp.float32
BF16 = jnp.bfloat16


def table(length):
    counter = np.arange(KM)
    freqs = np.where(counter < KM // 2, counter, counter - KM)
    angles = (np.arange(length)[:, None] * freqs[None, :] % length) * (2.0 * math.pi / length)
    return np.cos(angles), np.sin(angles)


def halves(values):
    values = np.asarray(values, np.float32)
    high = values.astype(BF16)
    return high, (values - high.astype(np.float32)).astype(BF16)


def split(values):
    high = values.astype(BF16)
    return high, (values - high.astype(F32)).astype(BF16)


def dot(left, right):
    return jnp.dot(left, right, preferred_element_type=F32)


def turn(values, sign):
    half = values.shape[-1] // 2
    return jnp.concatenate([-sign * values[..., half:], sign * values[..., :half]], axis=-1)


class Plan:
    def __init__(self, nx, ny, planes, rows_owned):
        self.nx, self.ny, self.planes = nx, ny, planes
        self.zb = min(8, planes)
        self.shares = max(1, KM // rows_owned)
        per_owner = max(1, rows_owned // KM)
        self.lane_groups = min(2, per_owner)
        self.owned_pairs = per_owner // self.lane_groups
        self.owners = KM // per_owner
        self.pairs = KM // self.lane_groups
        self.lanes = 2 * self.lane_groups * KM
        groups = self.lane_groups
        factor = 1.0 / math.sqrt(nx * ny * NZ)
        cos_x, sin_x = table(nx)
        cos_y, sin_y = table(ny)
        order = np.concatenate([np.arange(g, KM, groups) for g in range(groups)])
        cos_x, sin_x = cos_x[:, order], sin_x[:, order]
        from_real = np.concatenate([cos_x.T, -sin_x.T], 0) * factor
        from_imag = np.concatenate([sin_x.T, cos_x.T], 0) * factor
        self.fwd_x = np.stack(
            [np.concatenate(halves(from_real), 0), np.concatenate(halves(from_imag), 0)], 0
        )
        fwd_y = np.zeros((2, groups, ny, 2, groups, KM))
        inv_y = np.zeros((2, groups, KM, 2, groups, ny))
        for g in range(groups):
            fwd_y[0, g, :, 0, g] = cos_y
            fwd_y[0, g, :, 1, g] = -sin_y
            fwd_y[1, g, :, 0, g] = sin_y
            fwd_y[1, g, :, 1, g] = cos_y
            inv_y[0, g, :, 0, g] = cos_y.T
            inv_y[0, g, :, 1, g] = sin_y.T
            inv_y[1, g, :, 0, g] = -sin_y.T
            inv_y[1, g, :, 1, g] = cos_y.T
        fwd_y = fwd_y.reshape(2 * groups, ny, self.lanes)
        self.fwd_y = np.concatenate(halves(fwd_y), -1)
        inv_y = inv_y.reshape(self.lanes, 2 * groups * ny)
        inv_high, inv_low = halves(inv_y)
        self.inv_y = np.concatenate([inv_high, inv_high, inv_low], 0)
        inv_x = np.concatenate(
            [np.concatenate([cos_x, -sin_x], 1), np.concatenate([sin_x, cos_x], 1)], 0
        ) * factor
        high, low = halves(inv_x)
        self.inv_x = np.concatenate([high, high, low], 1)
        cos_z, sin_z = table(NZ)
        self.fwd_z = np.stack(halves(np.concatenate([cos_z, sin_z], 1)), 0)


def forward_kernel(plan, field, tab_x, tab_y, tab_z, out, along_x, along_xy):
    group = pl.program_id(1)
    rows = 2 * KM
    pairs, lanes, zb = plan.pairs, plan.lanes, plan.zb
    for z in range(zb):
        both = dot(tab_x[0], field[0, 0, z]) + dot(tab_x[1], field[1, 0, z])
        summed = both[:rows] + both[rows:]
        for part in range(plan.ny // 128):
            along_x[part, pl.ds(z, rows, stride=zb), :] = summed[:, part * 128 : part * 128 + 128]
    block = pairs * zb
    wide, narrow = 0.0, 0.0
    for g in range(rows // pairs):
        values = jnp.concatenate(
            [along_x[part, g * block : (g + 1) * block] for part in range(plan.ny // 128)], axis=1
        )
        high, low = split(values)
        wide = wide + dot(high, tab_y[g])
        narrow = narrow + dot(low, tab_y[g, :, :lanes])
    modes = wide[:, :lanes] + wide[:, lanes:] + narrow
    along_xy[:, pl.ds(pl.multiple_of(group * zb, zb), zb), :] = modes.reshape(pairs, zb, lanes)

    @pl.when(group == plan.planes // plan.zb - 1)
    def _():
        for pair in range(pairs):
            high, low = split(along_xy[pair])
            turned = dot(tab_z[0], high) + dot(tab_z[1], high) + dot(tab_z[0], low)
            out[pair // plan.owned_pairs, 0, pair % plan.owned_pairs] = turned[:KM] + turn(
                turned[KM:], -1.0
            )


def forward_modes(plan, field, tab_z):
    planes, nx, ny = plan.planes, plan.nx, plan.ny
    whole = lambda k, g: (0, 0, 0)
    return pl.pallas_call(
        functools.partial(forward_kernel, plan),
        grid=(3, planes // plan.zb),
        in_specs=[
            pl.BlockSpec((2, 1, plan.zb, nx, ny), lambda k, g: (0, k, g, 0, 0)),
            pl.BlockSpec(plan.fwd_x.shape, whole),
            pl.BlockSpec(plan.fwd_y.shape, whole),
            pl.BlockSpec((2, 2 * KM, planes), whole),
        ],
        out_specs=pl.BlockSpec(
            (plan.owners, 1, plan.owned_pairs, KM, plan.lanes), lambda k, g: (0, k, 0, 0, 0)
        ),
        out_shape=jax.ShapeDtypeStruct(
            (plan.owners, 3, plan.owned_pairs, KM, plan.lanes), F32
        ),
        scratch_shapes=[
            pltpu.VMEM((ny // 128, 2 * KM * plan.zb, 128), F32),
            pltpu.VMEM((plan.pairs, planes, plan.lanes), F32),
        ],
        compiler_params=pltpu.CompilerParams(vmem_limit_bytes=40 * 2**20),
        cost_estimate=pl.CostEstimate(
            flops=2 * 6 * planes * nx * ny * 128, bytes_accessed=12 * planes * nx * ny,
            transcendentals=0,
        ),
    )(field, jnp.asarray(plan.fwd_x), jnp.asarray(plan.fwd_y), tab_z)


def bypass_terms(weight, real, imag):
    s_r, s_i = weight[0], weight[4]
    v_r = [weight[1 + axis] for axis in range(3)]
    v_i = [weight[5 + axis] for axis in range(3)]
    outs_r, outs_i = [], []
    for k in range(3):
        a, b = (k + 1) % 3, (k + 2) % 3
        cross_r = (
            v_r[a] * real[b] - v_r[b] * real[a] + v_i[a] * imag[b] - v_i[b] * imag[a]
        )
        cross_i = (
            v_r[a] * imag[b] - v_r[b] * imag[a] - v_i[a] * real[b] + v_i[b] * real[a]
        )
        outs_r.append(s_r * real[k] + s_i * imag[k] - cross_i)
        outs_i.append(s_r * imag[k] - s_i * real[k] + cross_r)
    return outs_r, outs_i


def inverse_kernel(
    plan, step_planes, weight, field, modes, tab_z, tab_y, tab_x, out, along_z, along_zy, spectral
):
    step = pl.program_id(0)
    pairs, lanes, nx, ny, zb = plan.pairs, plan.lanes, plan.nx, plan.ny, plan.zb
    steps = zb // step_planes
    block = pairs * zb

    @pl.when(step == 0)
    def _():
        for pair in range(pairs):
            for k in range(3):
                values = modes[pair // plan.owned_pairs, k, pair % plan.owned_pairs]
                high, low = split(jnp.concatenate([values, turn(values, 1.0)], axis=0))
                along_z[k, pair] = dot(tab_z[0], high) + dot(tab_z[1], high) + dot(tab_z[0], low)

    @pl.when(step % steps == 0)
    def _():
        start = pl.multiple_of(step * step_planes, zb)
        for k in range(3):
            values = along_z[k, :, pl.ds(start, zb), :].reshape(block, lanes)
            high, low = split(values)
            parts = jnp.concatenate([high, low, high], axis=1)
            for g in range(2 * plan.lane_groups):
                result = dot(parts, tab_y[:, g * ny : (g + 1) * ny])
                for part in range(ny // 128):
                    along_zy[k, part, g * block : (g + 1) * block] = result[
                        :, part * 128 : part * 128 + 128
                    ]

    for z in range(step_planes):
        where = (step % steps) * step_planes + z
        for k in range(3):
            values = jnp.concatenate(
                [
                    along_zy[k, part, pl.ds(where, 2 * KM, stride=zb), :]
                    for part in range(ny // 128)
                ],
                axis=1,
            )
            high, low = split(values)
            spectral[z, k] = dot(tab_x[...], jnp.concatenate([high, low, high], axis=0))
        for row in range(0, nx, 16):
            for lane in range(0, ny, 128):
                rows, columns = pl.ds(row, 16), pl.ds(lane, 128)
                real = [field[k, z, rows, columns].astype(F32) for k in range(3)]
                imag = [field[3 + k, z, rows, columns].astype(F32) for k in range(3)]
                outs_r, outs_i = bypass_terms(weight, real, imag)
                for k in range(3):
                    out[k, z, rows, columns] = (outs_r[k] + spectral[z, k, rows, columns]).astype(
                        BF16
                    )
                    out[3 + k, z, rows, columns] = (
                        outs_i[k] + spectral[z, k, pl.ds(nx + row, 16), columns]
                    ).astype(BF16)


def inverse_field(plan, weight, field, modes, tab_z):
    planes, nx, ny = plan.planes, plan.nx, plan.ny
    step_planes = 2
    whole = lambda i: (0, 0)
    return pl.pallas_call(
        functools.partial(inverse_kernel, plan, step_planes),
        grid=(planes // step_planes,),
        in_specs=[
            pl.BlockSpec(memory_space=pltpu.SMEM),
            pl.BlockSpec((6, step_planes, nx, ny), lambda i: (0, i, 0, 0)),
            pl.BlockSpec(modes.shape, lambda i: (0, 0, 0, 0, 0)),
            pl.BlockSpec((2, planes, 2 * KM), lambda i: (0, 0, 0)),
            pl.BlockSpec(plan.inv_y.shape, whole),
            pl.BlockSpec(plan.inv_x.shape, whole),
        ],
        out_specs=pl.BlockSpec((6, step_planes, nx, ny), lambda i: (0, i, 0, 0)),
        out_shape=jax.ShapeDtypeStruct((6, planes, nx, ny), BF16),
        scratch_shapes=[
            pltpu.VMEM((3, plan.pairs, planes, plan.lanes), F32),
            pltpu.VMEM((3, ny // 128, 2 * KM * plan.zb, 128), F32),
            pltpu.VMEM((step_planes, 3, 2 * nx, ny), F32),
        ],
        compiler_params=pltpu.CompilerParams(vmem_limit_bytes=40 * 2**20),
        cost_estimate=pl.CostEstimate(
            flops=2 * 6 * planes * nx * ny * 192, bytes_accessed=24 * planes * nx * ny,
            transcendentals=0,
        ),
    )(weight, field, modes, tab_z, jnp.asarray(plan.inv_y), jnp.asarray(plan.inv_x))


def weight_terms(inputs_r, inputs_i, grads_r, grads_i):
    reals = [sum(inputs_r[k] * grads_r[k] + inputs_i[k] * grads_i[k] for k in range(3))]
    imags = [sum(inputs_r[k] * grads_i[k] - inputs_i[k] * grads_r[k] for k in range(3))]
    for k in range(3):
        a, b = (k + 1) % 3, (k + 2) % 3
        reals.append(
            inputs_r[a] * grads_i[b] - inputs_r[b] * grads_i[a]
            - inputs_i[a] * grads_r[b] + inputs_i[b] * grads_r[a]
        )
        imags.append(
            inputs_r[b] * grads_r[a] - inputs_r[a] * grads_r[b]
            + inputs_i[b] * grads_i[a] - inputs_i[a] * grads_i[b]
        )
    return reals, imags


def exchange_kernel(
    lines, grads, inputs, weights, modes, products,
    from_pair, pair_sum, from_line, mode_own,
    pair_send, pair_recv, line_send, line_recv, own_send, own_recv, pass_send, pass_recv,
):
    me = lax.axis_index("slab")
    side, place = lax.rem(me, 2), lax.div(me, 2)
    partner = me + 1 - 2 * side
    fields = (grads, inputs)
    half = grads.shape[-1] // 2

    def peer(step):
        return 2 * lax.rem(place + step, lines) + side

    barrier = pltpu.get_barrier_semaphore()
    pl.semaphore_signal(
        barrier, inc=1, device_id={"slab": partner}, device_id_type=pl.DeviceIdType.MESH
    )
    for step in range(1, lines):
        pl.semaphore_signal(
            barrier, inc=1, device_id={"slab": peer(step)}, device_id_type=pl.DeviceIdType.MESH
        )
    pl.semaphore_wait(barrier, lines)

    def send(source, target, send_sem, recv_sem, device):
        copy = pltpu.make_async_remote_copy(
            src_ref=source, dst_ref=target, send_sem=send_sem, recv_sem=recv_sem,
            device_id={"slab": device}, device_id_type=pl.DeviceIdType.MESH,
        )
        copy.start()
        return copy

    started = []

    def to_pair(f):
        return [
            send(
                fields[f].at[:, 1 - side, k], from_pair.at[f, k], pair_send.at[f, k],
                pair_recv.at[f, k], partner,
            )
            for k in range(3)
        ]

    def to_line(f, copies):
        sent = []
        for k in range(3):
            copies[k].wait_recv()
            pair_sum[f, k] = fields[f][:, side, k] + from_pair[f, k]
            sent.append([
                send(
                    pair_sum.at[f, k, lax.rem(place + step, lines)], from_line.at[f, k, step - 1],
                    line_send.at[f, k, step - 1], line_recv.at[f, k, step - 1], peer(step),
                )
                for step in range(1, lines)
            ])
        return sent

    def collect(f, sent):
        reals, imags = [], []
        for k in range(3):
            total = pair_sum[f, k, place]
            for step in range(1, lines):
                sent[k][step - 1].wait_recv()
                total = total + from_line[f, k, step - 1]
            reals.append(total[..., :half])
            imags.append(total[..., half:])
        return reals, imags

    grads_pair = to_pair(0)
    grads_line = to_line(0, grads_pair)
    inputs_pair = to_pair(1)
    grads_r, grads_i = collect(0, grads_line)
    mode_r, mode_i = bypass_terms(weights, grads_r, grads_i)
    for k in range(3):
        mode_own[k] = jnp.concatenate([mode_r[k], mode_i[k]], axis=-1)
    own = [
        send(mode_own, modes.at[me], own_send.at[step - 1], own_recv.at[step - 1], peer(step))
        for step in range(1, lines)
    ]
    passed = [send(mode_own, modes.at[me], pass_send.at[0], pass_recv.at[0], partner)]
    modes[me] = mode_own[...]
    inputs_line = to_line(1, inputs_pair)
    for step in range(1, lines):
        own[step - 1].wait_recv()
        block = modes.at[2 * lax.rem(place + lines - step, lines) + side]
        passed.append(send(block, block, pass_send.at[step], pass_recv.at[step], partner))
    inputs_r, inputs_i = collect(1, inputs_line)
    reals, imags = weight_terms(inputs_r, inputs_i, grads_r, grads_i)
    for term in range(4):
        products[term] = jnp.concatenate([reals[term], imags[term]], axis=-1)
    for copy in passed:
        copy.wait_recv()
    for copy in grads_pair + inputs_pair + own + passed + sum(grads_line + inputs_line, []):
        copy.wait_send()


def exchange(owners, grads, inputs, weights):
    lines = owners // 2
    kept = grads.shape[1:]
    block = kept[1:]
    sides = (lines, 2) + kept
    grads, inputs = grads.reshape(sides), inputs.reshape(sides)
    vmem = pl.BlockSpec(memory_space=pltpu.VMEM)
    dma = pltpu.SemaphoreType.DMA
    return pl.pallas_call(
        functools.partial(exchange_kernel, lines),
        in_specs=[vmem, vmem, vmem],
        out_specs=[vmem, vmem],
        out_shape=[
            jax.ShapeDtypeStruct((owners,) + kept, F32),
            jax.ShapeDtypeStruct((4,) + block, F32),
        ],
        scratch_shapes=[
            pltpu.VMEM((2, 3, lines) + block, F32),
            pltpu.VMEM((2, 3, lines) + block, F32),
            pltpu.VMEM((2, 3, lines - 1) + block, F32),
            pltpu.VMEM(kept, F32),
            dma((2, 3)), dma((2, 3)),
            dma((2, 3, lines - 1)), dma((2, 3, lines - 1)),
            dma((lines - 1,)), dma((lines - 1,)), dma((lines,)), dma((lines,)),
        ],
        compiler_params=pltpu.CompilerParams(
            collective_id=0, has_side_effects=True, vmem_limit_bytes=48 * 2**20
        ),
    )(grads, inputs, weights)


def shards(saved_input, output_grad, spectral_weight, bypass_weight):
    planes, nx, ny = saved_input.shape[3:]
    rows_owned = spectral_weight.shape[0]
    plan = Plan(nx, ny, planes, rows_owned)
    shares = plan.shares
    start = lax.axis_index("slab") * planes
    depth = lax.dynamic_slice_in_dim(jnp.asarray(plan.fwd_z), start, planes, axis=1)
    tab_fwd = jnp.swapaxes(depth, 1, 2)

    def partial_spectrum(field):
        parts = forward_modes(plan, field.reshape(2, 3, planes, nx, ny), tab_fwd)
        if shares > 1:
            parts = parts.reshape(plan.owners, 3, 1, KM, 2, shares, KM // shares)
            parts = jnp.transpose(parts, (0, 5, 1, 2, 3, 4, 6))
            parts = parts.reshape(plan.owners * shares, 3, 1, KM, plan.lanes // shares)
        return parts

    half = plan.lanes // (2 * shares)
    weights = spectral_weight.reshape(plan.owned_pairs, half, 8, KM)
    weights = jnp.transpose(weights, (2, 0, 3, 1))
    modes, products = exchange(
        plan.owners * shares, partial_spectrum(output_grad), partial_spectrum(saved_input), weights
    )
    if shares > 1:
        modes = modes.reshape(plan.owners, shares, 3, 1, KM, 2, KM // shares)
        modes = jnp.transpose(modes, (0, 2, 3, 4, 5, 1, 6))
        modes = modes.reshape(plan.owners, 3, 1, KM, plan.lanes)
    weight_grad = lax.psum(products, "rep")
    weight_grad = weight_grad.reshape(4, plan.owned_pairs, KM, 2, half)
    weight_grad = jnp.transpose(weight_grad, (1, 4, 3, 0, 2)).reshape(rows_owned, 8, 1, 1, KM)
    input_grad = inverse_field(
        plan, bypass_weight.reshape(8), output_grad.reshape(6, planes, nx, ny), modes, depth
    )
    return (input_grad.reshape(1, 6, 1, planes, nx, ny), weight_grad)


def solution(mesh):
    placed = (
        P("rep", None, None, "slab", None, None),
        P("rep", None, None, "slab", None, None),
        P("slab", None, None, None, None),
        P(),
    )
    return jax.shard_map(
        shards,
        mesh=mesh,
        in_specs=placed,
        out_specs=(P("rep", None, None, "slab", None, None), P("slab", None, None, None, None)),
        check_vma=False,
    )
```

```python
import functools
import math

import jax
import jax.numpy as jnp
import numpy as np
from jax import lax
from jax.experimental import pallas as pl
from jax.experimental.pallas import tpu as pltpu
from jax.sharding import PartitionSpec as P

NZ = 256
KM = 32
F32 = jnp.float32
BF16 = jnp.bfloat16


def table(length):
    counter = np.arange(KM)
    freqs = np.where(counter < KM // 2, counter, counter - KM)
    angles = (np.arange(length)[:, None] * freqs[None, :] % length) * (2.0 * math.pi / length)
    return np.cos(angles), np.sin(angles)


def halves(values):
    values = np.asarray(values, np.float32)
    high = values.astype(BF16)
    return high, (values - high.astype(np.float32)).astype(BF16)


def split(values):
    high = values.astype(BF16)
    return high, (values - high.astype(F32)).astype(BF16)


def dot(left, right):
    return jnp.dot(left, right, preferred_element_type=F32)


def turn(values, sign):
    half = values.shape[-1] // 2
    return jnp.concatenate([-sign * values[..., half:], sign * values[..., :half]], axis=-1)


class Plan:
    def __init__(self, nx, ny, planes, rows_owned):
        self.nx, self.ny, self.planes = nx, ny, planes
        self.zb = min(8, planes)
        self.shares = max(1, KM // rows_owned)
        per_owner = max(1, rows_owned // KM)
        self.lane_groups = min(2, per_owner)
        self.owned_pairs = per_owner // self.lane_groups
        self.owners = KM // per_owner
        self.pairs = KM // self.lane_groups
        self.lanes = 2 * self.lane_groups * KM
        groups = self.lane_groups
        factor = 1.0 / math.sqrt(nx * ny * NZ)
        cos_x, sin_x = table(nx)
        cos_y, sin_y = table(ny)
        order = np.concatenate([np.arange(g, KM, groups) for g in range(groups)])
        cos_x, sin_x = cos_x[:, order], sin_x[:, order]
        from_real = np.concatenate([cos_x.T, -sin_x.T], 0) * factor
        from_imag = np.concatenate([sin_x.T, cos_x.T], 0) * factor
        self.fwd_x = np.stack(
            [np.concatenate(halves(from_real), 0), np.concatenate(halves(from_imag), 0)], 0
        )
        fwd_y = np.zeros((2, groups, ny, 2, groups, KM))
        inv_y = np.zeros((2, groups, KM, 2, groups, ny))
        for g in range(groups):
            fwd_y[0, g, :, 0, g] = cos_y
            fwd_y[0, g, :, 1, g] = -sin_y
            fwd_y[1, g, :, 0, g] = sin_y
            fwd_y[1, g, :, 1, g] = cos_y
            inv_y[0, g, :, 0, g] = cos_y.T
            inv_y[0, g, :, 1, g] = sin_y.T
            inv_y[1, g, :, 0, g] = -sin_y.T
            inv_y[1, g, :, 1, g] = cos_y.T
        fwd_y = fwd_y.reshape(2 * groups, ny, self.lanes)
        self.fwd_y = np.concatenate(halves(fwd_y), -1)
        inv_y = inv_y.reshape(self.lanes, 2 * groups * ny)
        inv_high, inv_low = halves(inv_y)
        self.inv_y = np.concatenate([inv_high, inv_high, inv_low], 0)
        inv_x = np.concatenate(
            [np.concatenate([cos_x, -sin_x], 1), np.concatenate([sin_x, cos_x], 1)], 0
        ) * factor
        high, low = halves(inv_x)
        self.inv_x = np.concatenate([high, high, low], 1)
        cos_z, sin_z = table(NZ)
        self.fwd_z = np.stack(halves(np.concatenate([cos_z, sin_z], 1)), 0)


def forward_planes(plan, group, field, tab_x, tab_y, along_x, along_xy):
    rows = 2 * KM
    pairs, lanes, zb = plan.pairs, plan.lanes, plan.zb
    for z in range(zb):
        both = dot(tab_x[0], field[0, 0, z]) + dot(tab_x[1], field[1, 0, z])
        summed = both[:rows] + both[rows:]
        for part in range(plan.ny // 128):
            along_x[part, pl.ds(z, rows, stride=zb), :] = summed[:, part * 128 : part * 128 + 128]
    block = pairs * zb
    wide, narrow = 0.0, 0.0
    for g in range(rows // pairs):
        values = jnp.concatenate(
            [along_x[part, g * block : (g + 1) * block] for part in range(plan.ny // 128)], axis=1
        )
        high, low = split(values)
        wide = wide + dot(high, tab_y[g])
        narrow = narrow + dot(low, tab_y[g, :, :lanes])
    modes = wide[:, :lanes] + wide[:, lanes:] + narrow
    along_xy[:, pl.ds(pl.multiple_of(group * zb, zb), zb), :] = modes.reshape(pairs, zb, lanes)


def forward_depth(plan, tab_z, along_xy, store):
    for pair in range(plan.pairs):
        high, low = split(along_xy[pair])
        turned = dot(tab_z[0], high) + dot(tab_z[1], high) + dot(tab_z[0], low)
        store(
            pair // plan.owned_pairs, pair % plan.owned_pairs,
            turned[:KM] + turn(turned[KM:], -1.0),
        )


def forward_kernel(plan, field, tab_x, tab_y, tab_z, out, along_x, along_xy):
    group = pl.program_id(1)
    forward_planes(plan, group, field, tab_x, tab_y, along_x, along_xy)

    @pl.when(group == plan.planes // plan.zb - 1)
    def _():
        def store(owner, pair, values):
            out[owner, 0, pair] = values

        forward_depth(plan, tab_z, along_xy, store)


def forward_modes(plan, field, tab_z):
    planes, nx, ny = plan.planes, plan.nx, plan.ny
    whole = lambda k, g: (0, 0, 0)
    return pl.pallas_call(
        functools.partial(forward_kernel, plan),
        grid=(3, planes // plan.zb),
        in_specs=[
            pl.BlockSpec((2, 1, plan.zb, nx, ny), lambda k, g: (0, k, g, 0, 0)),
            pl.BlockSpec(plan.fwd_x.shape, whole),
            pl.BlockSpec(plan.fwd_y.shape, whole),
            pl.BlockSpec((2, 2 * KM, planes), whole),
        ],
        out_specs=pl.BlockSpec(
            (plan.owners, 1, plan.owned_pairs, KM, plan.lanes), lambda k, g: (0, k, 0, 0, 0)
        ),
        out_shape=jax.ShapeDtypeStruct(
            (plan.owners, 3, plan.owned_pairs, KM, plan.lanes), F32
        ),
        scratch_shapes=[
            pltpu.VMEM((ny // 128, 2 * KM * plan.zb, 128), F32),
            pltpu.VMEM((plan.pairs, planes, plan.lanes), F32),
        ],
        compiler_params=pltpu.CompilerParams(vmem_limit_bytes=40 * 2**20),
        cost_estimate=pl.CostEstimate(
            flops=2 * 6 * planes * nx * ny * 128, bytes_accessed=12 * planes * nx * ny,
            transcendentals=0,
        ),
    )(field, jnp.asarray(plan.fwd_x), jnp.asarray(plan.fwd_y), tab_z)


def bypass_terms(weight, real, imag):
    s_r, s_i = weight[0], weight[4]
    v_r = [weight[1 + axis] for axis in range(3)]
    v_i = [weight[5 + axis] for axis in range(3)]
    outs_r, outs_i = [], []
    for k in range(3):
        a, b = (k + 1) % 3, (k + 2) % 3
        cross_r = (
            v_r[a] * real[b] - v_r[b] * real[a] + v_i[a] * imag[b] - v_i[b] * imag[a]
        )
        cross_i = (
            v_r[a] * imag[b] - v_r[b] * imag[a] - v_i[a] * real[b] + v_i[b] * real[a]
        )
        outs_r.append(s_r * real[k] + s_i * imag[k] - cross_i)
        outs_i.append(s_r * imag[k] - s_i * real[k] + cross_r)
    return outs_r, outs_i


def inverse_kernel(
    plan, step_planes, weight, field, modes, tab_z, tab_y, tab_x, out, along_z, along_zy, spectral
):
    step = pl.program_id(0)
    pairs, lanes, nx, ny, zb = plan.pairs, plan.lanes, plan.nx, plan.ny, plan.zb
    steps = zb // step_planes
    block = pairs * zb

    @pl.when(step == 0)
    def _():
        for pair in range(pairs):
            for k in range(3):
                values = modes[pair // plan.owned_pairs, k, pair % plan.owned_pairs]
                high, low = split(jnp.concatenate([values, turn(values, 1.0)], axis=0))
                along_z[k, pair] = dot(tab_z[0], high) + dot(tab_z[1], high) + dot(tab_z[0], low)

    @pl.when(step % steps == 0)
    def _():
        start = pl.multiple_of(step * step_planes, zb)
        for k in range(3):
            values = along_z[k, :, pl.ds(start, zb), :].reshape(block, lanes)
            high, low = split(values)
            parts = jnp.concatenate([high, low, high], axis=1)
            for g in range(2 * plan.lane_groups):
                result = dot(parts, tab_y[:, g * ny : (g + 1) * ny])
                for part in range(ny // 128):
                    along_zy[k, part, g * block : (g + 1) * block] = result[
                        :, part * 128 : part * 128 + 128
                    ]

    for z in range(step_planes):
        where = (step % steps) * step_planes + z
        for k in range(3):
            values = jnp.concatenate(
                [
                    along_zy[k, part, pl.ds(where, 2 * KM, stride=zb), :]
                    for part in range(ny // 128)
                ],
                axis=1,
            )
            high, low = split(values)
            spectral[z, k] = dot(tab_x[...], jnp.concatenate([high, low, high], axis=0))
        for row in range(0, nx, 16):
            for lane in range(0, ny, 128):
                rows, columns = pl.ds(row, 16), pl.ds(lane, 128)
                real = [field[k, z, rows, columns].astype(F32) for k in range(3)]
                imag = [field[3 + k, z, rows, columns].astype(F32) for k in range(3)]
                outs_r, outs_i = bypass_terms(weight, real, imag)
                for k in range(3):
                    out[k, z, rows, columns] = (outs_r[k] + spectral[z, k, rows, columns]).astype(
                        BF16
                    )
                    out[3 + k, z, rows, columns] = (
                        outs_i[k] + spectral[z, k, pl.ds(nx + row, 16), columns]
                    ).astype(BF16)


def inverse_field(plan, weight, field, modes, tab_z):
    planes, nx, ny = plan.planes, plan.nx, plan.ny
    step_planes = 2
    whole = lambda i: (0, 0)
    return pl.pallas_call(
        functools.partial(inverse_kernel, plan, step_planes),
        grid=(planes // step_planes,),
        in_specs=[
            pl.BlockSpec(memory_space=pltpu.SMEM),
            pl.BlockSpec((6, step_planes, nx, ny), lambda i: (0, i, 0, 0)),
            pl.BlockSpec(modes.shape, lambda i: (0, 0, 0, 0, 0)),
            pl.BlockSpec((2, planes, 2 * KM), lambda i: (0, 0, 0)),
            pl.BlockSpec(plan.inv_y.shape, whole),
            pl.BlockSpec(plan.inv_x.shape, whole),
        ],
        out_specs=pl.BlockSpec((6, step_planes, nx, ny), lambda i: (0, i, 0, 0)),
        out_shape=jax.ShapeDtypeStruct((6, planes, nx, ny), BF16),
        scratch_shapes=[
            pltpu.VMEM((3, plan.pairs, planes, plan.lanes), F32),
            pltpu.VMEM((3, ny // 128, 2 * KM * plan.zb, 128), F32),
            pltpu.VMEM((step_planes, 3, 2 * nx, ny), F32),
        ],
        compiler_params=pltpu.CompilerParams(vmem_limit_bytes=40 * 2**20),
        cost_estimate=pl.CostEstimate(
            flops=2 * 6 * planes * nx * ny * 192, bytes_accessed=24 * planes * nx * ny,
            transcendentals=0,
        ),
    )(weight, field, modes, tab_z, jnp.asarray(plan.inv_y), jnp.asarray(plan.inv_x))


def weight_terms(inputs_r, inputs_i, grads_r, grads_i):
    reals = [sum(inputs_r[k] * grads_r[k] + inputs_i[k] * grads_i[k] for k in range(3))]
    imags = [sum(inputs_r[k] * grads_i[k] - inputs_i[k] * grads_r[k] for k in range(3))]
    for k in range(3):
        a, b = (k + 1) % 3, (k + 2) % 3
        reals.append(
            inputs_r[a] * grads_i[b] - inputs_r[b] * grads_i[a]
            - inputs_i[a] * grads_r[b] + inputs_i[b] * grads_r[a]
        )
        imags.append(
            inputs_r[b] * grads_r[a] - inputs_r[a] * grads_r[b]
            + inputs_i[b] * grads_i[a] - inputs_i[a] * grads_i[b]
        )
    return reals, imags


def exchange_kernel(
    lines, grads, inputs, weights, modes, products,
    from_pair, pair_sum, from_line, mode_own,
    pair_send, pair_recv, line_send, line_recv, own_send, own_recv, pass_send, pass_recv,
):
    me = lax.axis_index("slab")
    side, place = lax.rem(me, 2), lax.div(me, 2)
    partner = me + 1 - 2 * side
    fields = (grads, inputs)
    half = grads.shape[-1] // 2

    def peer(step):
        return 2 * lax.rem(place + step, lines) + side

    barrier = pltpu.get_barrier_semaphore()
    pl.semaphore_signal(
        barrier, inc=1, device_id={"slab": partner}, device_id_type=pl.DeviceIdType.MESH
    )
    for step in range(1, lines):
        pl.semaphore_signal(
            barrier, inc=1, device_id={"slab": peer(step)}, device_id_type=pl.DeviceIdType.MESH
        )
    pl.semaphore_wait(barrier, lines)

    def send(source, target, send_sem, recv_sem, device):
        copy = pltpu.make_async_remote_copy(
            src_ref=source, dst_ref=target, send_sem=send_sem, recv_sem=recv_sem,
            device_id={"slab": device}, device_id_type=pl.DeviceIdType.MESH,
        )
        copy.start()
        return copy

    started = []

    def to_pair(f):
        return [
            send(
                fields[f].at[:, 1 - side, k], from_pair.at[f, k], pair_send.at[f, k],
                pair_recv.at[f, k], partner,
            )
            for k in range(3)
        ]

    def to_line(f, copies):
        sent = []
        for k in range(3):
            copies[k].wait_recv()
            pair_sum[f, k] = fields[f][:, side, k] + from_pair[f, k]
            sent.append([
                send(
                    pair_sum.at[f, k, lax.rem(place + step, lines)], from_line.at[f, k, step - 1],
                    line_send.at[f, k, step - 1], line_recv.at[f, k, step - 1], peer(step),
                )
                for step in range(1, lines)
            ])
        return sent

    def collect(f, sent):
        reals, imags = [], []
        for k in range(3):
            total = pair_sum[f, k, place]
            for step in range(1, lines):
                sent[k][step - 1].wait_recv()
                total = total + from_line[f, k, step - 1]
            reals.append(total[..., :half])
            imags.append(total[..., half:])
        return reals, imags

    grads_pair = to_pair(0)
    grads_line = to_line(0, grads_pair)
    inputs_pair = to_pair(1)
    grads_r, grads_i = collect(0, grads_line)
    mode_r, mode_i = bypass_terms(weights, grads_r, grads_i)
    for k in range(3):
        mode_own[k] = jnp.concatenate([mode_r[k], mode_i[k]], axis=-1)
    own = [
        send(mode_own, modes.at[me], own_send.at[step - 1], own_recv.at[step - 1], peer(step))
        for step in range(1, lines)
    ]
    passed = [send(mode_own, modes.at[me], pass_send.at[0], pass_recv.at[0], partner)]
    modes[me] = mode_own[...]
    inputs_line = to_line(1, inputs_pair)
    for step in range(1, lines):
        own[step - 1].wait_recv()
        block = modes.at[2 * lax.rem(place + lines - step, lines) + side]
        passed.append(send(block, block, pass_send.at[step], pass_recv.at[step], partner))
    inputs_r, inputs_i = collect(1, inputs_line)
    reals, imags = weight_terms(inputs_r, inputs_i, grads_r, grads_i)
    for term in range(4):
        products[term] = jnp.concatenate([reals[term], imags[term]], axis=-1)
    for copy in passed:
        copy.wait_recv()
    for copy in grads_pair + inputs_pair + own + passed + sum(grads_line + inputs_line, []):
        copy.wait_send()


def merged_kernel(
    plan, lines, field, tab_x, tab_y, tab_z, grads, weights, modes_out, products,
    along_x, along_xy, inputs, modes, spectra,
    from_pair, pair_sum, from_line, mode_own,
    pair_send, pair_recv, line_send, line_recv, own_send, own_recv, pass_send, pass_recv,
):
    groups = plan.planes // plan.zb
    group = pl.program_id(1)
    step_now = pl.program_id(0) * groups + group
    last = 3 * groups - 1
    me = lax.axis_index("slab")
    side, place = lax.rem(me, 2), lax.div(me, 2)
    partner = me + 1 - 2 * side
    fields = (grads, inputs)
    half = plan.lanes // 2
    line_steps = range(1, lines)

    def peer(step):
        return 2 * lax.rem(place + step, lines) + side

    def copy(source, target, send_sem, recv_sem, device):
        return pltpu.make_async_remote_copy(
            src_ref=source, dst_ref=target, send_sem=send_sem, recv_sem=recv_sem,
            device_id={"slab": device}, device_id_type=pl.DeviceIdType.MESH,
        )

    def pair_copy(f, k):
        return copy(
            fields[f].at[:, 1 - side, k], from_pair.at[f, k], pair_send.at[f, k],
            pair_recv.at[f, k], partner,
        )

    def line_copy(f, k, step):
        return copy(
            pair_sum.at[f, k, lax.rem(place + step, lines)], from_line.at[f, k, step - 1],
            line_send.at[f, k, step - 1], line_recv.at[f, k, step - 1], peer(step),
        )

    def own_copy(step):
        return copy(
            mode_own, modes.at[me], own_send.at[step - 1], own_recv.at[step - 1], peer(step)
        )

    def pass_copy(step):
        if step == 0:
            return copy(mode_own, modes.at[me], pass_send.at[0], pass_recv.at[0], partner)
        block = modes.at[2 * lax.rem(place + lines - step, lines) + side]
        return copy(block, block, pass_send.at[step], pass_recv.at[step], partner)

    def to_line(f, k):
        pair_copy(f, k).wait_recv()
        pair_sum[f, k] = fields[f][:, side, k] + from_pair[f, k]
        for step in line_steps:
            line_copy(f, k, step).start()

    def collect(f):
        reals, imags = [], []
        for k in range(3):
            total = pair_sum[f, k, place]
            for step in line_steps:
                line_copy(f, k, step).wait_recv()
                total = total + from_line[f, k, step - 1]
            reals.append(total[..., :half])
            imags.append(total[..., half:])
        return reals, imags

    def join(real, imag):
        return jnp.concatenate([real, imag], axis=-1)

    def begin():
        barrier = pltpu.get_barrier_semaphore()
        for device in [partner] + [peer(step) for step in line_steps]:
            pl.semaphore_signal(
                barrier, inc=1, device_id={"slab": device}, device_id_type=pl.DeviceIdType.MESH
            )
        pl.semaphore_wait(barrier, lines)
        for k in range(3):
            pair_copy(0, k).start()

    def make_modes():
        grads_r, grads_i = collect(0)
        mode_r, mode_i = bypass_terms(weights, grads_r, grads_i)
        for k in range(3):
            spectra[k] = join(grads_r[k], grads_i[k])
            mode_own[k] = join(mode_r[k], mode_i[k])
        for step in line_steps:
            own_copy(step).start()
        pass_copy(0).start()
        modes[me] = mode_own[...]

    def pass_on():
        for step in line_steps:
            own_copy(step).wait_recv()
            pass_copy(step).start()

    def finish():
        inputs_r, inputs_i = collect(1)
        grads_r = [spectra[k, :, :, :half] for k in range(3)]
        grads_i = [spectra[k, :, :, half:] for k in range(3)]
        reals, imags = weight_terms(inputs_r, inputs_i, grads_r, grads_i)
        for term in range(4):
            products[term] = join(reals[term], imags[term])
        for step in range(lines):
            pass_copy(step).wait_recv()
        modes_out[...] = modes[...]
        for f in range(2):
            for k in range(3):
                pair_copy(f, k).wait_send()
                for step in line_steps:
                    line_copy(f, k, step).wait_send()
        for step in line_steps:
            own_copy(step).wait_send()
        for step in range(lines):
            pass_copy(step).wait_send()

    def at(twelfth, *stages):
        @pl.when(step_now == min(last, twelfth * groups // 4))
        def _():
            for stage in stages:
                stage()

    at(0, begin)
    forward_planes(plan, group, field, tab_x, tab_y, along_x, along_xy)

    for k in range(3):

        @pl.when(step_now == (k + 1) * groups - 1)
        def _(k=k):
            def store(owner, pair, values):
                inputs[owner // 2, owner % 2, k, pair] = values

            forward_depth(plan, tab_z, along_xy, store)
            pair_copy(1, k).start()

    at(2, lambda: to_line(0, 0))
    at(4, lambda: to_line(0, 1))
    at(6, lambda: to_line(0, 2))
    at(8, make_modes, lambda: to_line(1, 0))
    at(10, pass_on)
    at(12, lambda: to_line(1, 1), lambda: to_line(1, 2), finish)


def merged_exchange(plan, field, tab_z, grads, weights):
    planes, nx, ny, owners = plan.planes, plan.nx, plan.ny, plan.owners
    lines = owners // 2
    kept = grads.shape[1:]
    block = kept[1:]
    grads = grads.reshape((lines, 2) + kept)
    dma = pltpu.SemaphoreType.DMA

    def whole(shape):
        return pl.BlockSpec(shape, lambda k, g: (0,) * len(shape))

    return pl.pallas_call(
        functools.partial(merged_kernel, plan, lines),
        grid=(3, planes // plan.zb),
        in_specs=[
            pl.BlockSpec((2, 1, plan.zb, nx, ny), lambda k, g: (0, k, g, 0, 0)),
            whole(plan.fwd_x.shape),
            whole(plan.fwd_y.shape),
            whole((2, 2 * KM, planes)),
            whole(grads.shape),
            whole(weights.shape),
        ],
        out_specs=[whole((owners,) + kept), whole((4,) + block)],
        out_shape=[
            jax.ShapeDtypeStruct((owners,) + kept, F32),
            jax.ShapeDtypeStruct((4,) + block, F32),
        ],
        scratch_shapes=[
            pltpu.VMEM((ny // 128, 2 * KM * plan.zb, 128), F32),
            pltpu.VMEM((plan.pairs, planes, plan.lanes), F32),
            pltpu.VMEM(grads.shape, F32),
            pltpu.VMEM((owners,) + kept, F32),
            pltpu.VMEM(kept, F32),
            pltpu.VMEM((2, 3, lines) + block, F32),
            pltpu.VMEM((2, 3, lines) + block, F32),
            pltpu.VMEM((2, 3, lines - 1) + block, F32),
            pltpu.VMEM(kept, F32),
            dma((2, 3)), dma((2, 3)),
            dma((2, 3, lines - 1)), dma((2, 3, lines - 1)),
            dma((lines - 1,)), dma((lines - 1,)), dma((lines,)), dma((lines,)),
        ],
        compiler_params=pltpu.CompilerParams(
            collective_id=1, has_side_effects=True, vmem_limit_bytes=48 * 2**20
        ),
    )(field, jnp.asarray(plan.fwd_x), jnp.asarray(plan.fwd_y), tab_z, grads, weights)


def exchange(owners, grads, inputs, weights):
    lines = owners // 2
    kept = grads.shape[1:]
    block = kept[1:]
    sides = (lines, 2) + kept
    grads, inputs = grads.reshape(sides), inputs.reshape(sides)
    vmem = pl.BlockSpec(memory_space=pltpu.VMEM)
    dma = pltpu.SemaphoreType.DMA
    return pl.pallas_call(
        functools.partial(exchange_kernel, lines),
        in_specs=[vmem, vmem, vmem],
        out_specs=[vmem, vmem],
        out_shape=[
            jax.ShapeDtypeStruct((owners,) + kept, F32),
            jax.ShapeDtypeStruct((4,) + block, F32),
        ],
        scratch_shapes=[
            pltpu.VMEM((2, 3, lines) + block, F32),
            pltpu.VMEM((2, 3, lines) + block, F32),
            pltpu.VMEM((2, 3, lines - 1) + block, F32),
            pltpu.VMEM(kept, F32),
            dma((2, 3)), dma((2, 3)),
            dma((2, 3, lines - 1)), dma((2, 3, lines - 1)),
            dma((lines - 1,)), dma((lines - 1,)), dma((lines,)), dma((lines,)),
        ],
        compiler_params=pltpu.CompilerParams(
            collective_id=0, has_side_effects=True, vmem_limit_bytes=48 * 2**20
        ),
    )(grads, inputs, weights)


def shards(saved_input, output_grad, spectral_weight, bypass_weight):
    planes, nx, ny = saved_input.shape[3:]
    rows_owned = spectral_weight.shape[0]
    plan = Plan(nx, ny, planes, rows_owned)
    shares = plan.shares
    start = lax.axis_index("slab") * planes
    depth = lax.dynamic_slice_in_dim(jnp.asarray(plan.fwd_z), start, planes, axis=1)
    tab_fwd = jnp.swapaxes(depth, 1, 2)

    def partial_spectrum(field):
        parts = forward_modes(plan, field.reshape(2, 3, planes, nx, ny), tab_fwd)
        if shares > 1:
            parts = parts.reshape(plan.owners, 3, 1, KM, 2, shares, KM // shares)
            parts = jnp.transpose(parts, (0, 5, 1, 2, 3, 4, 6))
            parts = parts.reshape(plan.owners * shares, 3, 1, KM, plan.lanes // shares)
        return parts

    half = plan.lanes // (2 * shares)
    weights = spectral_weight.reshape(plan.owned_pairs, half, 8, KM)
    weights = jnp.transpose(weights, (2, 0, 3, 1))
    grads = partial_spectrum(output_grad)
    if shares == 1:
        field = saved_input.reshape(2, 3, planes, nx, ny)
        modes, products = merged_exchange(plan, field, tab_fwd, grads, weights)
    else:
        inputs = partial_spectrum(saved_input)
        modes, products = exchange(plan.owners * shares, grads, inputs, weights)
        modes = modes.reshape(plan.owners, shares, 3, 1, KM, 2, KM // shares)
        modes = jnp.transpose(modes, (0, 2, 3, 4, 5, 1, 6))
        modes = modes.reshape(plan.owners, 3, 1, KM, plan.lanes)
    weight_grad = lax.psum(products, "rep")
    weight_grad = weight_grad.reshape(4, plan.owned_pairs, KM, 2, half)
    weight_grad = jnp.transpose(weight_grad, (1, 4, 3, 0, 2)).reshape(rows_owned, 8, 1, 1, KM)
    input_grad = inverse_field(
        plan, bypass_weight.reshape(8), output_grad.reshape(6, planes, nx, ny), modes, depth
    )
    return (input_grad.reshape(1, 6, 1, planes, nx, ny), weight_grad)


def solution(mesh):
    placed = (
        P("rep", None, None, "slab", None, None),
        P("rep", None, None, "slab", None, None),
        P("slab", None, None, None, None),
        P(),
    )
    return jax.shard_map(
        shards,
        mesh=mesh,
        in_specs=placed,
        out_specs=(P("rep", None, None, "slab", None, None), P("slab", None, None, None, None)),
        check_vma=False,
    )
```
